256 devices in a mesh: group: 8 (over z), shard: 32 (over y, x, core).
Axes of the slice: x: 4, y: 4, z: 8, core: 2. Of those that a mesh axis runs over, the one named last changes fastest.
Arguments:
- queries: bfloat16 [32768, 4096], P('shard', 'group')
- neighbour_keys: bfloat16 [64, 128, 4096], P('shard', None, 'group')
- neighbour_values: bfloat16 [64, 128, 4096], P('shard', None, 'group'), may hold values from -6 to 6
- neighbours: int32 [512, 2], P('shard'), may hold values from 0 to 63, as said below
- out_weight: bfloat16 [4096, 4096], P('shard', 'group'), may hold values from -0.09375 to 0.09375
Outputs:
- mixed: bfloat16 [32768, 4096], P('shard', 'group')
The draws below stay inside these ranges and needn't reach their ends.
Inputs may be any that keep to these rules, and one draw needn't show every extreme that they name: Row c holds the ids of span c's two neighbours, two different ids; the owner of id n is n // 2. Among the ids in one device's rows (aligned blocks of 16 rows) at most 2 have one owner, and some owner is named exactly 2 times in every block.
All inputs are finite; a program needn't handle non-finite values.
Results may differ from the reference program's by a relative error of at most 0.0067.
Values may be sent and summed in bfloat16 or wider, within the bound.
No kernel may reach another device: no remote copies, remote signals or barrier semaphores. Data moves between devices by JAX's collectives and lax.ppermute only.
A program may use at most 128 MiB of HBM per device.

```python
import math
import jax
import jax.numpy as jnp
from jax import lax

D = 4096
HEADS = 32
HS = 128
SPAN = 64
NLEN = 128
NEIGH = 2
NB_DEV = 2
CH_DEV = 16
CAP = 2
TOKENS = 32768
SPANS = 512
NBR = 64
N_SHARD = 32


def neighbour_ids(key):
    key = jax.random.fold_in(key, 101)
    hot_key, block_key = jax.random.split(key)
    request_count = NEIGH * CH_DEV
    pool_size = N_SHARD * CAP
    hot_count = max(1, request_count // (2 * CAP))
    hot_order = jax.random.permutation(hot_key, N_SHARD)
    is_hot = (hot_order < hot_count).astype(jnp.int32)
    pool_owner = jnp.arange(pool_size, dtype=jnp.int32) // CAP

    def one_block(rand_key):
        score_key, shuffle_key, slot_key = jax.random.split(rand_key, 3)
        random_part = jax.random.randint(score_key, (pool_size,), 0, 4096, dtype=jnp.int32)
        scores = (random_part + 4096 * is_hot[pool_owner]) * 4096 + jnp.arange(pool_size, dtype=jnp.int32)
        chosen = lax.top_k(scores, request_count)[1]
        owners = (chosen // CAP).astype(jnp.int32)
        owners = jax.random.permutation(shuffle_key, owners).reshape(CH_DEV, NEIGH)
        local_slot = jax.random.randint(slot_key, (CH_DEV, NEIGH), 0, NB_DEV, dtype=jnp.int32)
        clash = (owners[:, 1] == owners[:, 0]) & (local_slot[:, 1] == local_slot[:, 0])
        second = jnp.where(clash, (local_slot[:, 0] + 1) % NB_DEV, local_slot[:, 1])
        local_slot = jnp.stack([local_slot[:, 0], second], axis=1)
        return owners * NB_DEV + local_slot
    blocks = jax.vmap(one_block)(jax.random.split(block_key, N_SHARD))
    return blocks.reshape(SPANS, NEIGH).astype(jnp.int32)


def keys_base(key):
    key = jax.random.fold_in(key, 202)
    drawn = jax.random.normal(key, (NBR, NLEN, HEADS * HS), jnp.float32)
    return jnp.clip(drawn, -6.0, 6.0)


def draw_neighbours(key, part):
    return neighbour_ids(key)


def draw_neighbour_keys(key, part):
    key_table = keys_base(key)
    return key_table.astype(jnp.bfloat16)


def draw_queries(key, part):
    key = jax.random.fold_in(key, 303)
    drawn_key = jax.random.fold_in(key, 0)
    drawn = jnp.clip(jax.random.normal(drawn_key, (TOKENS, HEADS * HS), jnp.float32), -6.0, 6.0)
    return drawn.astype(jnp.bfloat16)


def steps_of(own_key, dims, cuts, smallest, largest):
    loudness, own = 1.0, jax.random.fold_in(own_key, 6)
    for dim, blocks in cuts:
        draws = jnp.exp(jax.random.uniform(jax.random.fold_in(own, dim), (blocks,), jnp.float32, smallest / len(cuts), largest / len(cuts)))
        loudness = loudness * jnp.repeat(draws, dims[dim] // blocks).reshape([-1 if axis == dim else 1 for axis in range(len(dims))])
    return loudness


def noise(key, shape, spread, bound, pieces=(), kind=jnp.bfloat16):
    values = spread * jax.random.normal(key, shape, jnp.float32)
    if pieces:
        values = values * steps_of(key, shape, pieces, -0.22, 0.18)
    return jnp.clip(values, -bound, bound).astype(kind)


def setup_inputs(seed: int = 0) -> dict:
    keys = jax.random.split(jax.random.key(seed), 6)
    queries = draw_queries(jax.random.fold_in(keys[5], 71), 0)
    neighbour_keys = draw_neighbour_keys(jax.random.fold_in(keys[5], 71), 0)
    neighbour_values = noise(keys[2], (NBR, NLEN, HEADS * HS), 1.0, 6.0, ((0, 32), (2, 8)))
    neighbours = draw_neighbours(jax.random.fold_in(keys[5], 71), 0)
    out_weight = noise(keys[4], (HEADS * HS, D), (HEADS * HS) ** -0.5, 0.09375, ((0, 32), (1, 8)))
    return dict(queries=queries, neighbour_keys=neighbour_keys, neighbour_values=neighbour_values, neighbours=neighbours, out_weight=out_weight)


def attend_neighbour(query_rows, key_rows, value_rows):
    head_count = query_rows.shape[1] // HS
    score_scale = 1.0 / math.sqrt(HS)
    query_heads = query_rows.astype(jnp.float32).reshape(SPAN, head_count, HS)
    key_heads = key_rows.astype(jnp.float32).reshape(NLEN, head_count, HS)
    value_heads = value_rows.astype(jnp.float32).reshape(NLEN, head_count, HS)
    scores = jnp.einsum('qhd,khd->hqk', query_heads, key_heads) * score_scale
    row_top = lax.optimization_barrier(lax.optimization_barrier(jnp.max(scores, axis=2)).astype(jnp.bfloat16)).astype(jnp.float32)
    exp_scores = jnp.exp(scores - row_top[:, :, None])
    row_sum = lax.optimization_barrier(jnp.sum(exp_scores, axis=2))
    probs = lax.optimization_barrier(exp_scores.astype(jnp.bfloat16)).astype(jnp.float32)
    att_rows = jnp.einsum('hqk,khd->hqd', probs, value_heads) / row_sum[:, :, None]
    att_rows = lax.optimization_barrier(att_rows.astype(jnp.bfloat16)).astype(jnp.float32)
    row_sum_b = lax.optimization_barrier(row_sum.astype(jnp.bfloat16)).astype(jnp.float32)
    return (att_rows, row_top, row_sum_b)

def reference(queries, neighbour_keys, neighbour_values, neighbours, out_weight):
    feat_width = queries.shape[1]
    head_count = feat_width // HS
    span_query = queries.reshape(SPANS, SPAN, feat_width)

    def per_span(inputs):
        query_rows, neigh_ids = inputs
        results = []
        for neigh_idx in range(NEIGH):
            picked = neigh_ids[neigh_idx]
            results.append(attend_neighbour(query_rows, neighbour_keys[picked], neighbour_values[picked]))
        highest = results[0][1]
        for neigh_idx in range(1, NEIGH):
            highest = jnp.maximum(highest, results[neigh_idx][1])
        numer = jnp.zeros((head_count, SPAN, HS), jnp.float32)
        denom = jnp.zeros((head_count, SPAN), jnp.float32)
        for neigh_idx in range(NEIGH):
            att_rows, row_top, row_sum_b = results[neigh_idx]
            coeffs = row_sum_b * jnp.exp(row_top - highest)
            numer = numer + coeffs[:, :, None] * att_rows
            denom = denom + coeffs
        attended = (numer / denom[:, :, None]).astype(jnp.bfloat16)
        return attended.transpose(1, 0, 2).reshape(SPAN, head_count * HS)
    attended = lax.map(per_span, (span_query, neighbours)).reshape(TOKENS, feat_width)
    return jnp.dot(attended, out_weight, preferred_element_type=jnp.float32).astype(jnp.bfloat16)
```

```python
import functools
import math

import jax
import jax.numpy as jnp
from jax import lax
from jax.experimental import pallas as pl
from jax.experimental.pallas import tpu as pltpu
from jax.sharding import PartitionSpec as P

HS = 128
SPAN = 64
NX = 4
NY = 4
NCORE = 2


def plane_perm(move):
    pairs = []
    for y in range(NY):
        for x in range(NX):
            for c in range(NCORE):
                ty, tx, tc = move(y, x, c)
                src = (y * NX + x) * NCORE + c
                dst = ((ty % NY) * NX + tx % NX) * NCORE + tc
                pairs.append((src, dst))
    return pairs


def first_axis(step):
    return plane_perm(lambda y, x, c: (y, x + step, c) if c == 0 else (y + step, x, c))


def second_axis(step):
    return plane_perm(lambda y, x, c: (y + step, x, c) if c == 0 else (y, x + step, c))


def other_core():
    return plane_perm(lambda y, x, c: (y, x, 1 - c))


def send_plane(block, perm):
    return lax.ppermute(block, "shard", perm)


def send_group(block, step):
    count = lax.axis_size("group")
    return lax.ppermute(block, "group", [(i, (i + step) % count) for i in range(count)])


def ring_place(delta):
    return jnp.where(delta == 3, 1, jnp.where(delta == 0, 0, delta + 1))


def neighbour_codes(neighbours):
    shard = lax.axis_index("shard")
    my_y, my_x, my_core = shard // (NX * NCORE), (shard // NCORE) % NX, shard % NCORE
    owner, slot = neighbours // 2, neighbours % 2
    own_y, own_x, own_core = owner // (NX * NCORE), (owner // NCORE) % NX, owner % NCORE
    place_x = ring_place((own_x - my_x) & 3)
    place_y = ring_place((own_y - my_y) & 3)
    inner = jnp.where(own_core == 0, place_x, place_y)
    outer = jnp.where(own_core == 0, place_y, place_x)
    part = (own_core != my_core).astype(jnp.int32)
    return (((part * 4 + outer) * 4 + inner) * 2 + slot).reshape(-1)


def attend_kernel(span_count, codes, query_ref, *refs):
    tables = refs[:8]
    out_ref, table, sems = refs[8:]
    copies = [
        pltpu.make_async_copy(tables[i], table.at[pl.ds(i * 4, 4)], sems.at[i]) for i in range(8)
    ]
    for copy in copies:
        copy.start()
    for copy in copies:
        copy.wait()
    scale = math.log2(math.e) / math.sqrt(HS)
    for span in range(span_count):
        first, second = codes[2 * span], codes[2 * span + 1]
        place0, slot0 = first // 2, first % 2
        place1, slot1 = second // 2, second % 2
        keys = jnp.concatenate([table[place0, 0, slot0], table[place1, 0, slot1]], axis=0)
        values = jnp.concatenate([table[place0, 1, slot0], table[place1, 1, slot1]], axis=0)
        query = query_ref[pl.ds(span * SPAN, SPAN), :]
        scores = (
            lax.dot_general(
                query, keys, (((1,), (1,)), ((), ())), preferred_element_type=jnp.float32
            )
            * scale
        )
        top = jnp.max(scores, axis=1, keepdims=True)
        weights = jnp.exp2(scores - top)
        total = jnp.sum(weights, axis=1, keepdims=True)
        rows = jnp.dot(
            weights.astype(jnp.bfloat16), values, preferred_element_type=jnp.float32
        )
        out_ref[pl.ds(span * SPAN, SPAN), :] = (rows / total).astype(jnp.bfloat16)


def attend_head(queries, head, codes, tables):
    rows = queries.shape[0]
    return pl.pallas_call(
        functools.partial(attend_kernel, rows // SPAN),
        out_shape=jax.ShapeDtypeStruct((rows, HS), jnp.bfloat16),
        grid_spec=pltpu.PrefetchScalarGridSpec(
            num_scalar_prefetch=1,
            grid=(1,),
            in_specs=[pl.BlockSpec((rows, HS), lambda i, c: (0, head))]
            + [pl.BlockSpec(memory_space=pl.ANY)] * 8,
            out_specs=pl.BlockSpec((rows, HS), lambda i, c: (0, 0)),
            scratch_shapes=[
                pltpu.VMEM((32, 2, 2, 128, HS), jnp.bfloat16),
                pltpu.SemaphoreType.DMA((8,)),
            ],
        ),
        compiler_params=pltpu.CompilerParams(vmem_limit_bytes=24 * 1024 * 1024),
        cost_estimate=pl.CostEstimate(
            flops=4 * rows * 256 * HS, bytes_accessed=10_000_000, transcendentals=rows * 256
        ),
    )(codes, queries, *tables)


def project_kernel(count, has_acc, place, *refs):
    pieces = refs[:count]
    weights = refs[count : 2 * count]
    rest = refs[2 * count :]
    left = jnp.concatenate([p[...] for p in pieces], axis=1)
    right = jnp.concatenate([w[...] for w in weights], axis=0)
    total = jnp.dot(left, right, preferred_element_type=jnp.float32)
    if has_acc:
        total = total + rest[0][...]
    out_ref = rest[-1]
    out_ref[...] = total.astype(out_ref.dtype)


def project(pieces, heads, shifts, weight, acc, out_dtype):
    rows, cols = pieces[0].shape[0], weight.shape[1]
    count = len(pieces)
    groups = lax.axis_size("group")
    per_group = weight.shape[0] // HS // groups
    block = 256
    place = lax.axis_index("group").astype(jnp.int32).reshape(1)

    def weight_block(head, shift):
        return lambda i, p: (((p[0] - shift + groups) % groups) * per_group + head, 0)

    in_specs = [pl.BlockSpec((block, HS), lambda i, p: (i, 0)) for _ in pieces]
    in_specs += [
        pl.BlockSpec((HS, cols), weight_block(h, s)) for h, s in zip(heads, shifts)
    ]
    args = list(pieces) + [weight] * count
    if acc is not None:
        in_specs.append(pl.BlockSpec((block, cols), lambda i, p: (i, 0)))
        args.append(acc)
    return pl.pallas_call(
        functools.partial(project_kernel, count, acc is not None),
        out_shape=jax.ShapeDtypeStruct((rows, cols), out_dtype),
        grid_spec=pltpu.PrefetchScalarGridSpec(
            num_scalar_prefetch=1,
            grid=(rows // block,),
            in_specs=in_specs,
            out_specs=pl.BlockSpec((block, cols), lambda i, p: (i, 0)),
        ),
        compiler_params=pltpu.CompilerParams(vmem_limit_bytes=32 * 1024 * 1024),
        cost_estimate=pl.CostEstimate(
            flops=2 * rows * HS * count * cols,
            bytes_accessed=count * (rows + cols) * HS * 2 + rows * cols * 8,
            transcendentals=0,
        ),
    )(place, *args)


def gather_first(block):
    return [
        block,
        send_plane(block, first_axis(1)),
        send_plane(block, first_axis(-1)),
        send_plane(block, first_axis(2)),
    ]


def gather_second(row):
    mine = [
        row,
        send_plane(row, second_axis(1)),
        send_plane(row, second_axis(-1)),
        send_plane(row, second_axis(2)),
    ]
    swap = other_core()
    return mine + [send_plane(part, swap) for part in mine]


def ring_group(block, last_right):
    pieces, shifts = [block], [0]
    right = left = block
    for step in range(1, 4):
        right = send_group(right, 1)
        left = send_group(left, -1)
        pieces += [right, left]
        shifts += [step, -step]
    pieces.append(send_group(right, 1) if last_right else send_group(left, -1))
    shifts.append(4)
    return pieces, shifts


def after(value, earlier):
    return lax.optimization_barrier((value, *earlier))[0]


def per_device(queries, neighbour_keys, neighbour_values, neighbours, out_weight):
    heads = queries.shape[1] // HS
    codes = neighbour_codes(neighbours)

    def packed(head):
        cols = slice(head * HS, (head + 1) * HS)
        return jnp.stack([neighbour_keys[:, :, cols], neighbour_values[:, :, cols]])

    first = gather_first(packed(0))
    weight = lax.all_gather(out_weight, "shard", axis=0, tiled=True)
    pieces, piece_heads, shifts = [], [], []
    tables, all_rows = [], []
    for head in range(heads):
        if head == 0:
            row = jnp.stack(first)
        else:
            if head == 1:
                block = jnp.stack([packed(h) for h in range(1, heads)])
                later = gather_first(after(block, tables[1:4]))
            row = jnp.stack([part[head - 1] for part in later])
            row = after(row, tables[1:4] + all_rows[-1:])
        tables = gather_second(row)
        rows = attend_head(queries, head, codes, tables)
        all_rows.append(rows)
        got, places = ring_group(rows, head % 2 == 0)
        pieces.append(got)
        piece_heads.append([head] * len(got))
        shifts.append(places)
    acc = project(
        sum(pieces[:-1], []),
        sum(piece_heads[:-1], []),
        sum(shifts[:-1], []),
        weight,
        None,
        jnp.float32,
    )
    return project(pieces[-1], piece_heads[-1], shifts[-1], weight, acc, jnp.bfloat16)


def solution(mesh):
    in_specs = (
        P("shard", "group"),
        P("shard", None, "group"),
        P("shard", None, "group"),
        P("shard", None),
        P("shard", "group"),
    )
    out_specs = P("shard", "group")
    return jax.shard_map(
        per_device, mesh=mesh, in_specs=in_specs, out_specs=out_specs, check_vma=False
    )
```

```python
import functools
import math

import jax
import jax.numpy as jnp
from jax import lax
from jax.experimental import pallas as pl
from jax.experimental.pallas import tpu as pltpu
from jax.sharding import PartitionSpec as P

HS = 128
SPAN = 64
NLEN = 128
NX = 4
NY = 4
NCORE = 2
GROUPS = 8


def plane_perm(move):
    pairs = []
    for y in range(NY):
        for x in range(NX):
            for c in range(NCORE):
                ty, tx, tc = move(y, x, c)
                src = (y * NX + x) * NCORE + c
                dst = ((ty % NY) * NX + tx % NX) * NCORE + tc
                pairs.append((src, dst))
    return pairs


def first_axis(step):
    return plane_perm(lambda y, x, c: (y, x + step, c) if c == 0 else (y + step, x, c))


def second_axis(step):
    return plane_perm(lambda y, x, c: (y + step, x, c) if c == 0 else (y, x + step, c))


def other_core():
    return plane_perm(lambda y, x, c: (y, x, 1 - c))


def send_plane(block, perm):
    return lax.ppermute(block, "shard", perm)


def send_group(block, step):
    count = lax.axis_size("group")
    return lax.ppermute(block, "group", [(i, (i + step) % count) for i in range(count)])


def ring_place(delta):
    return jnp.where(delta == 3, 1, jnp.where(delta == 0, 0, delta + 1))


def neighbour_codes(neighbours):
    shard = lax.axis_index("shard")
    my_y, my_x, my_core = shard // (NX * NCORE), (shard // NCORE) % NX, shard % NCORE
    owner, slot = neighbours // 2, neighbours % 2
    own_y, own_x, own_core = owner // (NX * NCORE), (owner // NCORE) % NX, owner % NCORE
    place_x = ring_place((own_x - my_x) & 3)
    place_y = ring_place((own_y - my_y) & 3)
    inner = jnp.where(own_core == 0, place_x, place_y)
    outer = jnp.where(own_core == 0, place_y, place_x)
    part = (own_core != my_core).astype(jnp.int32)
    return (((part * 4 + outer) * 4 + inner) * 2 + slot).reshape(-1)


def pack_kernel(sub, *refs):
    sources, (out_ref, sems) = refs[:-2], refs[-2:]
    copies = []
    for i, source in enumerate(sources):
        size = source.shape[0]
        piece = source if sub is None else source.at[:, sub]
        copies.append(
            pltpu.make_async_copy(piece, out_ref.at[pl.ds(i * size, size)], sems.at[i])
        )
    for copy in copies:
        copy.start()
    for copy in copies:
        copy.wait()


def pack(parts, sub=None):
    shape = parts[0].shape[1 if sub is None else 2 :]
    shape = (len(parts) * parts[0].shape[0],) + shape
    return pl.pallas_call(
        functools.partial(pack_kernel, sub),
        out_shape=jax.ShapeDtypeStruct(shape, parts[0].dtype),
        in_specs=[pl.BlockSpec(memory_space=pl.ANY)] * len(parts),
        out_specs=pl.BlockSpec(memory_space=pltpu.VMEM),
        scratch_shapes=[pltpu.SemaphoreType.DMA((len(parts),))],
        compiler_params=pltpu.CompilerParams(vmem_limit_bytes=4 * 1024 * 1024),
    )(*parts)


def attend_spans(span_count, query_ref, out_ref, scores_ref, pick):
    for span in range(span_count):
        rows = pl.ds(span * SPAN, SPAN)
        for i in range(2):
            scores_ref[rows, pl.ds(i * NLEN, NLEN)] = lax.dot_general(
                query_ref[rows, :],
                pick(span, i, 0),
                (((1,), (1,)), ((), ())),
                preferred_element_type=jnp.float32,
            )
    for span in range(span_count):
        rows = pl.ds(span * SPAN, SPAN)
        found = []
        for i in range(2):
            scores = scores_ref[rows, pl.ds(i * NLEN, NLEN)] * (1.0 / math.sqrt(HS))
            top = jnp.max(scores, axis=1, keepdims=True)
            top = top.astype(jnp.bfloat16).astype(jnp.float32)
            weights = jnp.exp(scores - top)
            total = jnp.sum(weights, axis=1, keepdims=True)
            part = jnp.dot(
                weights.astype(jnp.bfloat16), pick(span, i, 1), preferred_element_type=jnp.float32
            )
            part = (part / total).astype(jnp.bfloat16).astype(jnp.float32)
            found.append((part, top, total.astype(jnp.bfloat16).astype(jnp.float32)))
        (part0, top0, total0), (part1, top1, total1) = found
        highest = jnp.maximum(top0, top1)
        coeff0 = total0 * jnp.exp(top0 - highest)
        coeff1 = total1 * jnp.exp(top1 - highest)
        merged = (coeff0 * part0 + coeff1 * part1) / (coeff0 + coeff1)
        out_ref[rows, :] = merged.astype(jnp.bfloat16)


def attend_kernel(span_count, codes, query_ref, own_ref, other_ref, out_ref, scores_ref):
    def pick(span, neighbour, kind):
        code = codes[2 * span + neighbour]
        place, slot = lax.rem(code // 2, 16), lax.rem(code, 2)
        return jnp.where(code < 32, own_ref[place, kind, slot], other_ref[place, kind, slot])

    attend_spans(span_count, query_ref, out_ref, scores_ref, pick)


def attend_owned_kernel(span_count, codes, query_ref, owned_ref, out_ref, scores_ref, table, sems):
    copies = [
        pltpu.make_async_copy(
            owned_ref.at[pl.ds(i * 4, 4)], table.at[pl.ds(i * 4, 4)], sems.at[i]
        )
        for i in range(8)
    ]
    for copy in copies:
        copy.start()
    for copy in copies:
        copy.wait()

    def pick(span, neighbour, kind):
        code = codes[2 * span + neighbour]
        return table[code // 2, kind, lax.rem(code, 2)]

    attend_spans(span_count, query_ref, out_ref, scores_ref, pick)


def attend_head(queries, head, codes, tables):
    rows = queries.shape[0]
    scratch = [pltpu.VMEM((rows, 2 * NLEN), jnp.float32)]
    if len(tables) == 2:
        kernel, space = attend_kernel, pltpu.VMEM
    else:
        kernel, space = attend_owned_kernel, pl.ANY
        shape = tables[0].shape
        scratch += [pltpu.VMEM(shape, jnp.bfloat16), pltpu.SemaphoreType.DMA((8,))]
    return pl.pallas_call(
        functools.partial(kernel, rows // SPAN),
        out_shape=jax.ShapeDtypeStruct((rows, HS), jnp.bfloat16),
        grid_spec=pltpu.PrefetchScalarGridSpec(
            num_scalar_prefetch=1,
            grid=(1,),
            in_specs=[pl.BlockSpec((rows, HS), lambda i, c: (0, head))]
            + [pl.BlockSpec(memory_space=space)] * len(tables),
            out_specs=pl.BlockSpec((rows, HS), lambda i, c: (0, 0)),
            scratch_shapes=scratch,
        ),
        compiler_params=pltpu.CompilerParams(vmem_limit_bytes=12 * 1024 * 1024),
        cost_estimate=pl.CostEstimate(
            flops=4 * rows * 256 * HS, bytes_accessed=10_000_000, transcendentals=rows * 256
        ),
    )(codes, queries, *tables)


def project_kernel(head, has_acc, place, *refs):
    refs, out_ref = refs[:-1], refs[-1]
    acc_ref, refs = (refs[-1], refs[:-1]) if has_acc else (None, refs)
    pieces, weight = refs[:-1], refs[-1]
    per_group = weight.shape[0] // GROUPS
    if len(pieces) == 1:
        left = jnp.concatenate([pieces[0][g] for g in range(GROUPS)], axis=1)
        right = jnp.concatenate([weight[g * per_group + head] for g in range(GROUPS)], axis=0)
    else:
        left = jnp.concatenate([p[...] for p in pieces], axis=1)
        groups = [lax.rem(place[0] - shift + GROUPS, GROUPS) for shift in RING_SHIFTS]
        right = jnp.concatenate([weight[g * per_group + head] for g in groups], axis=0)
    total = jnp.dot(left, right, preferred_element_type=jnp.float32)
    if has_acc:
        total = total + acc_ref[...]
    out_ref[...] = total.astype(out_ref.dtype)


def project(pieces, head, weight, acc, out_dtype):
    rows, cols = pieces[0].shape[-2], weight.shape[2]
    block = 256
    place = lax.axis_index("group").astype(jnp.int32).reshape(1)
    if len(pieces) == 1:
        in_specs = [pl.BlockSpec((GROUPS, block, HS), lambda i, p: (0, i, 0))]
    else:
        in_specs = [pl.BlockSpec((block, HS), lambda i, p: (i, 0)) for _ in pieces]
    in_specs.append(pl.BlockSpec(memory_space=pltpu.VMEM))
    args = list(pieces) + [weight]
    if acc is not None:
        in_specs.append(pl.BlockSpec((block, cols), lambda i, p: (i, 0)))
        args.append(acc)
    return pl.pallas_call(
        functools.partial(project_kernel, head, acc is not None),
        out_shape=jax.ShapeDtypeStruct((rows, cols), out_dtype),
        grid_spec=pltpu.PrefetchScalarGridSpec(
            num_scalar_prefetch=1,
            grid=(rows // block,),
            in_specs=in_specs,
            out_specs=pl.BlockSpec((block, cols), lambda i, p: (i, 0)),
        ),
        compiler_params=pltpu.CompilerParams(vmem_limit_bytes=12 * 1024 * 1024),
        cost_estimate=pl.CostEstimate(
            flops=2 * rows * HS * 8 * cols,
            bytes_accessed=8 * (rows + cols) * HS * 2 + rows * cols * 8,
            transcendentals=0,
        ),
    )(place, *args)


def gather_first(block):
    return [
        block,
        send_plane(block, first_axis(1)),
        send_plane(block, first_axis(-1)),
        send_plane(block, first_axis(2)),
    ]


def gather_second(row):
    return [
        row,
        send_plane(row, second_axis(1)),
        send_plane(row, second_axis(-1)),
        send_plane(row, second_axis(2)),
    ]


def after(value, earlier):
    return lax.optimization_barrier((value, *earlier))[0]


RING_SHIFTS = (0, 1, -1, 2, -2, 3, -3, 4)


class GroupRing:
    def __init__(self, block, last_right):
        self.pieces = [block]
        self.right = self.left = block
        self.last_right = last_right
        self.step = 0

    def advance(self, earlier=()):
        self.step += 1
        right, left = after(self.right, earlier), after(self.left, earlier)
        if self.step < 4:
            self.right, self.left = send_group(right, 1), send_group(left, -1)
            got = [self.right, self.left]
        else:
            got = [send_group(right, 1) if self.last_right else send_group(left, -1)]
        self.pieces += got
        return got


def per_device(queries, neighbour_keys, neighbour_values, neighbours, out_weight):
    codes = neighbour_codes(neighbours)

    def packed(head):
        cols = slice(head * HS, (head + 1) * HS)
        return jnp.stack([neighbour_keys[:, :, cols], neighbour_values[:, :, cols]])

    parts = gather_first(jnp.stack([packed(h) for h in range(3)]))
    row0 = jnp.stack([part[0] for part in parts])
    row12 = jnp.stack([part[1:] for part in parts])
    owned = lax.all_gather(packed(3), "shard", axis=0, tiled=False)
    swap = other_core()

    own0 = pack(gather_second(row0))
    other0 = send_plane(own0, swap)
    weight = lax.all_gather(after(out_weight, [own0]), "shard", axis=0, tiled=False)
    parts12 = gather_second(after(row12, [own0]))
    rows0 = attend_head(queries, 0, codes, [own0, other0])
    ring0 = GroupRing(rows0, True)
    ring0.advance()
    step02 = ring0.advance()
    step03 = ring0.advance()
    plain = neighbours.reshape(-1)
    rows3 = attend_head(after(queries, step02), 3, plain, [owned])
    ring3 = GroupRing(rows3, False)
    parts12 = [after(part, step03 + [rows3]) for part in parts12]
    own1 = pack(parts12, 0)
    other1 = send_plane(own1, swap)
    own2 = pack([after(part, [own1]) for part in parts12], 1)
    other2 = send_plane(own2, swap)
    step04 = ring0.advance()
    step31 = ring3.advance()
    rows1 = attend_head(queries, 1, codes, [own1, other1])
    ring1 = GroupRing(rows1, True)
    step11 = ring1.advance()
    rows2 = attend_head(after(queries, [rows1] + step31), 2, codes, [own2, other2])
    ring2 = GroupRing(rows2, False)
    step21 = ring2.advance()
    step32 = ring3.advance()
    step12 = ring1.advance()
    step22 = ring2.advance(step32)
    step33 = ring3.advance()
    step13 = ring1.advance()
    step34 = ring3.advance()
    acc = project(ring0.pieces, 0, weight, None, jnp.float32)
    step23 = ring2.advance(step33 + [acc])
    step14 = ring1.advance()
    acc = project(ring3.pieces, 3, weight, acc, jnp.float32)
    step24 = ring2.advance()
    acc = project(ring1.pieces, 1, weight, acc, jnp.float32)
    return project(ring2.pieces, 2, weight, acc, jnp.bfloat16)


def solution(mesh):
    in_specs = (
        P("shard", "group"),
        P("shard", None, "group"),
        P("shard", None, "group"),
        P("shard", None),
        P("shard", "group"),
    )
    out_specs = P("shard", "group")
    return jax.shard_map(
        per_device, mesh=mesh, in_specs=in_specs, out_specs=out_specs, check_vma=False
    )
```

```python
import functools
import math

import jax
import jax.numpy as jnp
from jax import lax
from jax.experimental import pallas as pl
from jax.experimental.pallas import tpu as pltpu
from jax.sharding import PartitionSpec as P

HS = 128
SPAN = 64
NLEN = 128
NX = 4
NY = 4
NCORE = 2
GROUPS = 8


def plane_perm(move):
    pairs = []
    for y in range(NY):
        for x in range(NX):
            for c in range(NCORE):
                ty, tx, tc = move(y, x, c)
                src = (y * NX + x) * NCORE + c
                dst = ((ty % NY) * NX + tx % NX) * NCORE + tc
                pairs.append((src, dst))
    return pairs


def first_axis(step):
    return plane_perm(lambda y, x, c: (y, x + step, c) if c == 0 else (y + step, x, c))


def second_axis(step):
    return plane_perm(lambda y, x, c: (y + step, x, c) if c == 0 else (y, x + step, c))


def other_core():
    return plane_perm(lambda y, x, c: (y, x, 1 - c))


def send_plane(block, perm):
    return lax.ppermute(block, "shard", perm)


def send_group(block, step):
    count = lax.axis_size("group")
    return lax.ppermute(block, "group", [(i, (i + step) % count) for i in range(count)])


def ring_place(delta):
    return jnp.where(delta == 3, 1, jnp.where(delta == 0, 0, delta + 1))


def neighbour_codes(neighbours):
    shard = lax.axis_index("shard")
    my_y, my_x, my_core = shard // (NX * NCORE), (shard // NCORE) % NX, shard % NCORE
    owner, slot = neighbours // 2, neighbours % 2
    own_y, own_x, own_core = owner // (NX * NCORE), (owner // NCORE) % NX, owner % NCORE
    place_x = ring_place((own_x - my_x) & 3)
    place_y = ring_place((own_y - my_y) & 3)
    inner = jnp.where(own_core == 0, place_x, place_y)
    outer = jnp.where(own_core == 0, place_y, place_x)
    part = (own_core != my_core).astype(jnp.int32)
    return (((part * 4 + outer) * 4 + inner) * 2 + slot).reshape(-1)


def pack_kernel(sub, *refs):
    sources, (out_ref, sems) = refs[:-2], refs[-2:]
    copies = []
    for i, source in enumerate(sources):
        size = source.shape[0]
        piece = source if sub is None else source.at[:, sub]
        copies.append(
            pltpu.make_async_copy(piece, out_ref.at[pl.ds(i * size, size)], sems.at[i])
        )
    for copy in copies:
        copy.start()
    for copy in copies:
        copy.wait()


def pack(parts, sub=None):
    shape = parts[0].shape[1 if sub is None else 2 :]
    shape = (len(parts) * parts[0].shape[0],) + shape
    return pl.pallas_call(
        functools.partial(pack_kernel, sub),
        out_shape=jax.ShapeDtypeStruct(shape, parts[0].dtype),
        in_specs=[pl.BlockSpec(memory_space=pl.ANY)] * len(parts),
        out_specs=pl.BlockSpec(memory_space=pltpu.VMEM),
        scratch_shapes=[pltpu.SemaphoreType.DMA((len(parts),))],
        compiler_params=pltpu.CompilerParams(vmem_limit_bytes=4 * 1024 * 1024),
    )(*parts)


def attend_spans(span_count, query_ref, out_ref, scores_ref, pick):
    for span in range(span_count):
        rows = pl.ds(span * SPAN, SPAN)
        for i in range(2):
            scores_ref[rows, pl.ds(i * NLEN, NLEN)] = lax.dot_general(
                query_ref[rows, :],
                pick(span, i, 0),
                (((1,), (1,)), ((), ())),
                preferred_element_type=jnp.float32,
            )
    for span in range(span_count):
        rows = pl.ds(span * SPAN, SPAN)
        found = []
        for i in range(2):
            scores = scores_ref[rows, pl.ds(i * NLEN, NLEN)] * (1.0 / math.sqrt(HS))
            top = jnp.max(scores, axis=1, keepdims=True)
            top = top.astype(jnp.bfloat16).astype(jnp.float32)
            weights = jnp.exp(scores - top)
            total = jnp.sum(weights, axis=1, keepdims=True)
            part = jnp.dot(
                weights.astype(jnp.bfloat16), pick(span, i, 1), preferred_element_type=jnp.float32
            )
            part = (part / total).astype(jnp.bfloat16).astype(jnp.float32)
            found.append((part, top, total.astype(jnp.bfloat16).astype(jnp.float32)))
        (part0, top0, total0), (part1, top1, total1) = found
        highest = jnp.maximum(top0, top1)
        coeff0 = total0 * jnp.exp(top0 - highest)
        coeff1 = total1 * jnp.exp(top1 - highest)
        merged = (coeff0 * part0 + coeff1 * part1) / (coeff0 + coeff1)
        out_ref[rows, :] = merged.astype(jnp.bfloat16)


def attend_kernel(span_count, codes, query_ref, own_ref, other_ref, out_ref, scores_ref):
    def pick(span, neighbour, kind):
        code = codes[2 * span + neighbour]
        place, slot = lax.rem(code // 2, 16), lax.rem(code, 2)
        return jnp.where(code < 32, own_ref[place, kind, slot], other_ref[place, kind, slot])

    attend_spans(span_count, query_ref, out_ref, scores_ref, pick)


def attend_owned_kernel(span_count, codes, query_ref, owned_ref, out_ref, scores_ref, table, sems):
    copies = [
        pltpu.make_async_copy(
            owned_ref.at[pl.ds(i * 2, 2), 0], table.at[pl.ds(i * 2, 2)], sems.at[i]
        )
        for i in range(16)
    ]
    for copy in copies:
        copy.start()
    for copy in copies:
        copy.wait()

    def pick(span, neighbour, kind):
        code = codes[2 * span + neighbour]
        return table[code // 2, kind, lax.rem(code, 2)]

    attend_spans(span_count, query_ref, out_ref, scores_ref, pick)


def attend_head(queries, head, codes, tables):
    rows = queries.shape[0]
    scratch = [pltpu.VMEM((rows, 2 * NLEN), jnp.float32)]
    grant = 12 if len(tables) == 2 else 56
    if len(tables) == 2:
        kernel, space = attend_kernel, pltpu.VMEM
    else:
        kernel, space = attend_owned_kernel, pltpu.HBM
        shape = tables[0].shape
        scratch += [pltpu.VMEM(shape[:1] + shape[2:], jnp.bfloat16), pltpu.SemaphoreType.DMA((16,))]
    return pl.pallas_call(
        functools.partial(kernel, rows // SPAN),
        out_shape=jax.ShapeDtypeStruct((rows, HS), jnp.bfloat16),
        grid_spec=pltpu.PrefetchScalarGridSpec(
            num_scalar_prefetch=1,
            grid=(1,),
            in_specs=[pl.BlockSpec((rows, HS), lambda i, c: (0, head))]
            + [pl.BlockSpec(memory_space=space)] * len(tables),
            out_specs=pl.BlockSpec((rows, HS), lambda i, c: (0, 0)),
            scratch_shapes=scratch,
        ),
        compiler_params=pltpu.CompilerParams(vmem_limit_bytes=grant * 1024 * 1024),
        cost_estimate=pl.CostEstimate(
            flops=4 * rows * 256 * HS, bytes_accessed=10_000_000, transcendentals=rows * 256
        ),
    )(codes, queries, *tables)


def arrange_kernel(owned_ref, out_ref, sems):
    copies = [
        pltpu.make_async_copy(
            owned_ref.at[pl.ds(i * 8, 8), 1, j // 2, j % 2],
            out_ref.at[pl.ds(i * 8, 8), :, pl.ds(j * HS, HS)],
            sems.at[i, j],
        )
        for i in range(4)
        for j in range(4)
    ]
    for copy in copies:
        copy.start()
    for copy in copies:
        copy.wait()


def arrange(owned):
    return pl.pallas_call(
        arrange_kernel,
        out_shape=jax.ShapeDtypeStruct((owned.shape[0], HS, 4 * HS), jnp.bfloat16),
        in_specs=[pl.BlockSpec(memory_space=pltpu.HBM)],
        out_specs=pl.BlockSpec(memory_space=pltpu.VMEM),
        scratch_shapes=[pltpu.SemaphoreType.DMA((4, 4))],
        compiler_params=pltpu.CompilerParams(vmem_limit_bytes=56 * 1024 * 1024),
    )(owned)


def project_kernel(head, has_acc, place, *refs):
    refs, out_ref = refs[:-1], refs[-1]
    acc_ref, refs = (refs[-1], refs[:-1]) if has_acc else (None, refs)
    pieces, weight = refs[:-1], refs[-1]
    per_group = weight.shape[0] // GROUPS
    if len(pieces) == 1:
        left = jnp.concatenate([pieces[0][g] for g in range(GROUPS)], axis=1)
        right = jnp.concatenate([weight[g * per_group + head] for g in range(GROUPS)], axis=0)
    else:
        left = jnp.concatenate([p[...] for p in pieces], axis=1)
        groups = [lax.rem(place[0] - shift + GROUPS, GROUPS) for shift in RING_SHIFTS]
        right = jnp.concatenate([weight[g * per_group + head] for g in groups], axis=0)
    total = jnp.dot(left, right, preferred_element_type=jnp.float32)
    if has_acc:
        total = total + acc_ref[...]
    out_ref[...] = total.astype(out_ref.dtype)


def project(pieces, head, weight, acc, out_dtype):
    rows, cols = pieces[0].shape[-2], weight.shape[2]
    block = 256
    place = lax.axis_index("group").astype(jnp.int32).reshape(1)
    if len(pieces) == 1:
        in_specs = [pl.BlockSpec((GROUPS, block, HS), lambda i, p: (0, i, 0))]
    else:
        in_specs = [pl.BlockSpec((block, HS), lambda i, p: (i, 0)) for _ in pieces]
    in_specs.append(pl.BlockSpec(memory_space=pltpu.VMEM))
    args = list(pieces) + [weight]
    if acc is not None:
        in_specs.append(pl.BlockSpec((block, cols), lambda i, p: (i, 0)))
        args.append(acc)
    return pl.pallas_call(
        functools.partial(project_kernel, head, acc is not None),
        out_shape=jax.ShapeDtypeStruct((rows, cols), out_dtype),
        grid_spec=pltpu.PrefetchScalarGridSpec(
            num_scalar_prefetch=1,
            grid=(rows // block,),
            in_specs=in_specs,
            out_specs=pl.BlockSpec((block, cols), lambda i, p: (i, 0)),
        ),
        compiler_params=pltpu.CompilerParams(vmem_limit_bytes=12 * 1024 * 1024),
        cost_estimate=pl.CostEstimate(
            flops=2 * rows * HS * 8 * cols,
            bytes_accessed=8 * (rows + cols) * HS * 2 + rows * cols * 8,
            transcendentals=0,
        ),
    )(place, *args)


def gather_first(block):
    return [
        block,
        send_plane(block, first_axis(1)),
        send_plane(block, first_axis(-1)),
        send_plane(block, first_axis(2)),
    ]


def gather_second(row):
    return [
        row,
        send_plane(row, second_axis(1)),
        send_plane(row, second_axis(-1)),
        send_plane(row, second_axis(2)),
    ]


def after(value, earlier):
    return lax.optimization_barrier((value, *earlier))[0]


RING_SHIFTS = (0, 1, -1, 2, -2, 3, -3, 4)


class GroupRing:
    def __init__(self, block, last_right):
        self.pieces = [block]
        self.right = self.left = block
        self.last_right = last_right
        self.step = 0

    def advance(self, earlier=()):
        self.step += 1
        right, left = after(self.right, earlier), after(self.left, earlier)
        if self.step < 4:
            self.right, self.left = send_group(right, 1), send_group(left, -1)
            got = [self.right, self.left]
        else:
            got = [send_group(right, 1) if self.last_right else send_group(left, -1)]
        self.pieces += got
        return got


def per_device(queries, neighbour_keys, neighbour_values, neighbours, out_weight):
    codes = neighbour_codes(neighbours)

    def packed(head):
        cols = slice(head * HS, (head + 1) * HS)
        return jnp.stack([neighbour_keys[:, :, cols], neighbour_values[:, :, cols]])

    parts = gather_first(jnp.stack([packed(h) for h in range(3)]))
    row0 = jnp.stack([part[0] for part in parts])
    row12 = jnp.stack([part[1:] for part in parts])
    weight = jnp.stack([out_weight[:, i * HS : (i + 1) * HS] for i in range(4)])
    block = jnp.stack([packed(3), weight.reshape(2, 2, HS, HS)])
    swap = other_core()

    own0 = pack(gather_second(row0))
    owned = lax.all_gather(after(block, [own0]), "shard", axis=0, tiled=False)
    other0 = send_plane(own0, swap)
    parts12 = gather_second(after(row12, [own0]))
    rows0 = attend_head(queries, 0, codes, [own0, other0])
    ring0 = GroupRing(rows0, True)
    ring0.advance()
    step02 = ring0.advance()
    parts12 = [after(part, step02) for part in parts12]
    own1 = pack(parts12, 0)
    other1 = send_plane(own1, swap)
    own2 = pack([after(part, [own1]) for part in parts12], 1)
    other2 = send_plane(own2, swap)
    step03 = ring0.advance()
    rows1 = attend_head(queries, 1, codes, [own1, other1])
    ring1 = GroupRing(rows1, True)
    step11 = ring1.advance()
    rows2 = attend_head(after(queries, [rows1]), 2, codes, [own2, other2])
    ring2 = GroupRing(rows2, False)
    step21 = ring2.advance()
    step04 = ring0.advance()
    step12 = ring1.advance(step03)
    plain = neighbours.reshape(-1)
    rows3 = attend_head(after(queries, step21 + step11), 3, plain, [owned])
    ring3 = GroupRing(rows3, False)
    step22 = ring2.advance()
    step31 = ring3.advance()
    weight = arrange(after(owned, [rows3]))
    acc = project(ring0.pieces, 0, weight, None, jnp.float32)
    step13 = ring1.advance()
    step32 = ring3.advance()
    step23 = ring2.advance(step31)
    step14 = ring1.advance()
    step33 = ring3.advance(step13 + [acc])
    step24 = ring2.advance()
    acc = project(ring1.pieces, 1, weight, acc, jnp.float32)
    step34 = ring3.advance([acc])
    acc = project(ring2.pieces, 2, weight, acc, jnp.float32)
    return project(ring3.pieces, 3, weight, acc, jnp.bfloat16)


def solution(mesh):
    in_specs = (
        P("shard", "group"),
        P("shard", None, "group"),
        P("shard", None, "group"),
        P("shard", None),
        P("shard", "group"),
    )
    out_specs = P("shard", "group")
    return jax.shard_map(
        per_device, mesh=mesh, in_specs=in_specs, out_specs=out_specs, check_vma=False
    )
```

```python
import functools
import math

import jax
import jax.numpy as jnp
from jax import lax
from jax.experimental import pallas as pl
from jax.experimental.pallas import tpu as pltpu
from jax.sharding import PartitionSpec as P

HS = 128
SPAN = 64
NLEN = 128
NX = 4
NY = 4
NCORE = 2
GROUPS = 8


def plane_perm(move):
    pairs = []
    for y in range(NY):
        for x in range(NX):
            for c in range(NCORE):
                ty, tx, tc = move(y, x, c)
                src = (y * NX + x) * NCORE + c
                dst = ((ty % NY) * NX + tx % NX) * NCORE + tc
                pairs.append((src, dst))
    return pairs


def first_axis(step):
    return plane_perm(lambda y, x, c: (y, x + step, c) if c == 0 else (y + step, x, c))


def second_axis(step):
    return plane_perm(lambda y, x, c: (y + step, x, c) if c == 0 else (y, x + step, c))


def other_core():
    return plane_perm(lambda y, x, c: (y, x, 1 - c))


def send_plane(block, perm):
    return lax.ppermute(block, "shard", perm)


def send_group(block, step):
    count = lax.axis_size("group")
    return lax.ppermute(block, "group", [(i, (i + step) % count) for i in range(count)])


def ring_place(delta):
    return jnp.where(delta == 3, 1, jnp.where(delta == 0, 0, delta + 1))


def neighbour_codes(neighbours):
    shard = lax.axis_index("shard")
    my_y, my_x, my_core = shard // (NX * NCORE), (shard // NCORE) % NX, shard % NCORE
    owner, slot = neighbours // 2, neighbours % 2
    own_y, own_x, own_core = owner // (NX * NCORE), (owner // NCORE) % NX, owner % NCORE
    place_x = ring_place((own_x - my_x) & 3)
    place_y = ring_place((own_y - my_y) & 3)
    inner = jnp.where(own_core == 0, place_x, place_y)
    outer = jnp.where(own_core == 0, place_y, place_x)
    part = (own_core != my_core).astype(jnp.int32)
    return (((part * 4 + outer) * 4 + inner) * 2 + slot).reshape(-1)


def pack_kernel(sub, *refs):
    sources, (out_ref, sems) = refs[:-2], refs[-2:]
    copies = []
    for i, source in enumerate(sources):
        size = source.shape[0]
        piece = source if sub is None else source.at[:, sub]
        copies.append(
            pltpu.make_async_copy(piece, out_ref.at[pl.ds(i * size, size)], sems.at[i])
        )
    for copy in copies:
        copy.start()
    for copy in copies:
        copy.wait()


def pack(parts, sub=None):
    shape = parts[0].shape[1 if sub is None else 2 :]
    shape = (len(parts) * parts[0].shape[0],) + shape
    return pl.pallas_call(
        functools.partial(pack_kernel, sub),
        out_shape=jax.ShapeDtypeStruct(shape, parts[0].dtype),
        in_specs=[pl.BlockSpec(memory_space=pl.ANY)] * len(parts),
        out_specs=pl.BlockSpec(memory_space=pltpu.VMEM),
        scratch_shapes=[pltpu.SemaphoreType.DMA((len(parts),))],
        compiler_params=pltpu.CompilerParams(vmem_limit_bytes=4 * 1024 * 1024),
    )(*parts)


def attend_spans(span_count, query_ref, out_ref, scores_ref, pick):
    for span in range(span_count):
        rows = pl.ds(span * SPAN, SPAN)
        for i in range(2):
            scores_ref[rows, pl.ds(i * NLEN, NLEN)] = lax.dot_general(
                query_ref[rows, :],
                pick(span, i, 0),
                (((1,), (1,)), ((), ())),
                preferred_element_type=jnp.float32,
            )
    for span in range(span_count):
        rows = pl.ds(span * SPAN, SPAN)
        found = []
        for i in range(2):
            scores = scores_ref[rows, pl.ds(i * NLEN, NLEN)] * (1.0 / math.sqrt(HS))
            top = jnp.max(scores, axis=1, keepdims=True)
            top = top.astype(jnp.bfloat16).astype(jnp.float32)
            weights = jnp.exp(scores - top)
            total = jnp.sum(weights, axis=1, keepdims=True)
            part = jnp.dot(
                weights.astype(jnp.bfloat16), pick(span, i, 1), preferred_element_type=jnp.float32
            )
            part = (part / total).astype(jnp.bfloat16).astype(jnp.float32)
            found.append((part, top, total.astype(jnp.bfloat16).astype(jnp.float32)))
        (part0, top0, total0), (part1, top1, total1) = found
        highest = jnp.maximum(top0, top1)
        coeff0 = total0 * jnp.exp(top0 - highest)
        coeff1 = total1 * jnp.exp(top1 - highest)
        merged = (coeff0 * part0 + coeff1 * part1) / (coeff0 + coeff1)
        out_ref[rows, :] = merged.astype(jnp.bfloat16)


def attend_kernel(span_count, codes, query_ref, own_ref, other_ref, out_ref, scores_ref):
    def pick(span, neighbour, kind):
        code = codes[2 * span + neighbour]
        place, slot = lax.rem(code // 2, 16), lax.rem(code, 2)
        return jnp.where(code < 32, own_ref[place, kind, slot], other_ref[place, kind, slot])

    attend_spans(span_count, query_ref, out_ref, scores_ref, pick)


def attend_owned_kernel(span_count, codes, query_ref, owned_ref, out_ref, scores_ref, table, sems):
    copies = [
        pltpu.make_async_copy(
            owned_ref.at[pl.ds(i * 2, 2), 0], table.at[pl.ds(i * 2, 2)], sems.at[i]
        )
        for i in range(16)
    ]
    for copy in copies:
        copy.start()
    for copy in copies:
        copy.wait()

    def pick(span, neighbour, kind):
        code = codes[2 * span + neighbour]
        return table[code // 2, kind, lax.rem(code, 2)]

    attend_spans(span_count, query_ref, out_ref, scores_ref, pick)


def attend_head(queries, head, codes, tables):
    rows = queries.shape[0]
    scratch = [pltpu.VMEM((rows, 2 * NLEN), jnp.float32)]
    grant = 12 if len(tables) == 2 else 56
    if len(tables) == 2:
        kernel, space = attend_kernel, pltpu.VMEM
    else:
        kernel, space = attend_owned_kernel, pltpu.HBM
        shape = tables[0].shape
        scratch += [pltpu.VMEM(shape[:1] + shape[2:], jnp.bfloat16), pltpu.SemaphoreType.DMA((16,))]
    return pl.pallas_call(
        functools.partial(kernel, rows // SPAN),
        out_shape=jax.ShapeDtypeStruct((rows, HS), jnp.bfloat16),
        grid_spec=pltpu.PrefetchScalarGridSpec(
            num_scalar_prefetch=1,
            grid=(1,),
            in_specs=[pl.BlockSpec((rows, HS), lambda i, c: (0, head))]
            + [pl.BlockSpec(memory_space=space)] * len(tables),
            out_specs=pl.BlockSpec((rows, HS), lambda i, c: (0, 0)),
            scratch_shapes=scratch,
        ),
        compiler_params=pltpu.CompilerParams(vmem_limit_bytes=grant * 1024 * 1024),
        cost_estimate=pl.CostEstimate(
            flops=4 * rows * 256 * HS, bytes_accessed=10_000_000, transcendentals=rows * 256
        ),
    )(codes, queries, *tables)


def arrange_kernel(owned_ref, out_ref, sems):
    copies = [
        pltpu.make_async_copy(
            owned_ref.at[pl.ds(i * 8, 8), 1, j // 2, j % 2],
            out_ref.at[pl.ds(i * 8, 8), :, pl.ds(j * HS, HS)],
            sems.at[i, j],
        )
        for i in range(4)
        for j in range(4)
    ]
    for copy in copies:
        copy.start()
    for copy in copies:
        copy.wait()


def arrange(owned):
    return pl.pallas_call(
        arrange_kernel,
        out_shape=jax.ShapeDtypeStruct((owned.shape[0], HS, 4 * HS), jnp.bfloat16),
        in_specs=[pl.BlockSpec(memory_space=pltpu.HBM)],
        out_specs=pl.BlockSpec(memory_space=pltpu.VMEM),
        scratch_shapes=[pltpu.SemaphoreType.DMA((4, 4))],
        compiler_params=pltpu.CompilerParams(vmem_limit_bytes=56 * 1024 * 1024),
    )(owned)


def project_kernel(head, has_acc, place, *refs):
    refs, out_ref = refs[:-1], refs[-1]
    acc_ref, refs = (refs[-1], refs[:-1]) if has_acc else (None, refs)
    pieces, weight = refs[:-1], refs[-1]
    per_group = weight.shape[0] // GROUPS
    if len(pieces) == 1:
        left = jnp.concatenate([pieces[0][g] for g in range(GROUPS)], axis=1)
        right = jnp.concatenate([weight[g * per_group + head] for g in range(GROUPS)], axis=0)
    else:
        left = jnp.concatenate([p[...] for p in pieces], axis=1)
        groups = [lax.rem(place[0] - shift + GROUPS, GROUPS) for shift in RING_SHIFTS]
        right = jnp.concatenate([weight[g * per_group + head] for g in groups], axis=0)
    total = jnp.dot(left, right, preferred_element_type=jnp.float32)
    if has_acc:
        total = total + acc_ref[...]
    out_ref[...] = total.astype(out_ref.dtype)


def project(pieces, head, weight, acc, out_dtype):
    rows, cols = pieces[0].shape[-2], weight.shape[2]
    block = 256
    place = lax.axis_index("group").astype(jnp.int32).reshape(1)
    if len(pieces) == 1:
        in_specs = [pl.BlockSpec((GROUPS, block, HS), lambda i, p: (0, i, 0))]
    else:
        in_specs = [pl.BlockSpec((block, HS), lambda i, p: (i, 0)) for _ in pieces]
    in_specs.append(pl.BlockSpec(memory_space=pltpu.VMEM))
    args = list(pieces) + [weight]
    if acc is not None:
        in_specs.append(pl.BlockSpec((block, cols), lambda i, p: (i, 0)))
        args.append(acc)
    return pl.pallas_call(
        functools.partial(project_kernel, head, acc is not None),
        out_shape=jax.ShapeDtypeStruct((rows, cols), out_dtype),
        grid_spec=pltpu.PrefetchScalarGridSpec(
            num_scalar_prefetch=1,
            grid=(rows // block,),
            in_specs=in_specs,
            out_specs=pl.BlockSpec((block, cols), lambda i, p: (i, 0)),
        ),
        compiler_params=pltpu.CompilerParams(vmem_limit_bytes=12 * 1024 * 1024),
        cost_estimate=pl.CostEstimate(
            flops=2 * rows * HS * 8 * cols,
            bytes_accessed=8 * (rows + cols) * HS * 2 + rows * cols * 8,
            transcendentals=0,
        ),
    )(place, *args)


def gather_first(block):
    return [
        block,
        send_plane(block, first_axis(1)),
        send_plane(block, first_axis(-1)),
        send_plane(block, first_axis(2)),
    ]


def gather_second(row):
    return [
        row,
        send_plane(row, second_axis(1)),
        send_plane(row, second_axis(-1)),
        send_plane(row, second_axis(2)),
    ]


def after(value, earlier):
    return lax.optimization_barrier((value, *earlier))[0]


RING_SHIFTS = (0, 1, -1, 2, -2, 3, -3, 4)


class GroupRing:
    def __init__(self, block, last_right):
        self.pieces = [block]
        self.right = self.left = block
        self.last_right = last_right
        self.step = 0

    def advance(self, earlier=()):
        self.step += 1
        right, left = after(self.right, earlier), after(self.left, earlier)
        if self.step < 4:
            self.right, self.left = send_group(right, 1), send_group(left, -1)
            got = [self.right, self.left]
        else:
            got = [send_group(right, 1) if self.last_right else send_group(left, -1)]
        self.pieces += got
        return got


def per_device(queries, neighbour_keys, neighbour_values, neighbours, out_weight):
    codes = neighbour_codes(neighbours)

    def packed(head):
        cols = slice(head * HS, (head + 1) * HS)
        return jnp.stack([neighbour_keys[:, :, cols], neighbour_values[:, :, cols]])

    parts = gather_first(jnp.stack([packed(h) for h in range(3)]))
    row0 = jnp.stack([part[0] for part in parts])
    row12 = jnp.stack([part[1:] for part in parts])
    weight = jnp.stack([out_weight[:, i * HS : (i + 1) * HS] for i in range(4)])
    block = jnp.stack([packed(3), weight.reshape(2, 2, HS, HS)])
    swap = other_core()

    own0 = pack(gather_second(row0))
    owned = lax.all_gather(after(block, [own0]), "shard", axis=0, tiled=False)
    other0 = send_plane(own0, swap)
    parts12 = gather_second(after(row12, [own0]))
    rows0 = attend_head(queries, 0, codes, [own0, other0])
    ring0 = GroupRing(rows0, True)
    ring0.advance()
    step02 = ring0.advance()
    parts12 = [after(part, step02) for part in parts12]
    own1 = pack(parts12, 0)
    other1 = send_plane(own1, swap)
    own2 = pack([after(part, [own1]) for part in parts12], 1)
    other2 = send_plane(own2, swap)
    step03 = ring0.advance()
    rows1 = attend_head(queries, 1, codes, [own1, other1])
    ring1 = GroupRing(rows1, False)
    step11 = ring1.advance()
    rows2 = attend_head(after(queries, [rows1]), 2, codes, [own2, other2])
    ring2 = GroupRing(rows2, False)
    step21 = ring2.advance()
    step04 = ring0.advance()
    step12 = ring1.advance(step03)
    plain = neighbours.reshape(-1)
    rows3 = attend_head(after(queries, step21 + step11), 3, plain, [owned])
    ring3 = GroupRing(rows3, True)
    step22 = ring2.advance()
    step31 = ring3.advance()
    weight = arrange(after(owned, [rows3]))
    acc = project(ring0.pieces, 0, weight, None, jnp.float32)
    step13 = ring1.advance()
    step32 = ring3.advance()
    step23 = ring2.advance(step31)
    step14 = ring1.advance()
    step33 = ring3.advance(step13 + [acc])
    step24 = ring2.advance()
    acc = project(ring1.pieces, 1, weight, acc, jnp.float32)
    step34 = ring3.advance([acc])
    acc = project(ring2.pieces, 2, weight, acc, jnp.float32)
    return project(ring3.pieces, 3, weight, acc, jnp.bfloat16)


def solution(mesh):
    in_specs = (
        P("shard", "group"),
        P("shard", None, "group"),
        P("shard", None, "group"),
        P("shard", None),
        P("shard", "group"),
    )
    out_specs = P("shard", "group")
    return jax.shard_map(
        per_device, mesh=mesh, in_specs=in_specs, out_specs=out_specs, check_vma=False
    )
```
